128 devices in a mesh: grid: 8 (over x, core), mesh: 16 (over y, z).
Axes of the slice: x: 4, y: 4, z: 4, core: 2. Of those that a mesh axis runs over, the one named last changes fastest.
Arguments:
- grid_inputs: bfloat16 [393216, 227], P(('grid', 'mesh')), may hold values from -6 to 6
- embed_weight: bfloat16 [227, 512], replicated, may hold values from -0.375 to 0.375
- send_weight: bfloat16 [512, 512], replicated, may hold values from -0.25 to 0.25
- g2m_dest: int32 [3072, 3], P(('grid', 'mesh')), may hold values from 0 to 63, all different within a row
- g2m_edges: bfloat16 [3072, 3, 128, 128], P(('grid', 'mesh')), may hold values from -0.3125 to 0.3125
- encode_weight: bfloat16 [512, 512], replicated, may hold values from -0.25 to 0.25
- adj_codes: int32 [16, 32, 4], P('grid', 'mesh'), may hold values from 0 to 8
- adj_count: int32 [16, 32], P('grid', 'mesh'), may hold values from 1 to 4
- couplings: bfloat16 [16, 32, 4, 128, 128], P('grid', 'mesh'), may hold values from -0.25 to 0.25
- message_weight: bfloat16 [2, 512, 512], replicated, may hold values from -0.25 to 0.25
- node_weight: bfloat16 [2, 512, 512], replicated, may hold values from -0.25 to 0.25
- decode_weight: bfloat16 [512, 512], replicated, may hold values from -0.25 to 0.25
- m2g_src: int32 [3072, 3], P(('grid', 'mesh')), may hold values from 0 to 63, all different within a row
- m2g_edges: bfloat16 [3072, 3, 128, 128], P(('grid', 'mesh')), may hold values from -0.3125 to 0.3125
- output_weight: bfloat16 [512, 227], replicated, may hold values from -0.25 to 0.25
Outputs:
- prediction: bfloat16 [393216, 227], P(('grid', 'mesh'))
The draws below stay inside these ranges and needn't reach their ends.
Inputs may be any that keep to these rules, and one draw needn't show every extreme that they name: `g2m_dest`: each row names 3 different codes; code c is patch row c // 32 of the block's band and column c % 32. `m2g_src`: each row names 3 different codes, read as for g2m_dest. `adj_codes`: codes may repeat within a patch.
All inputs are finite; a program needn't handle non-finite values.
Results may differ from the reference program's by a relative error of at most 0.027.
Values may be sent and summed in bfloat16 or wider, within the bound.
No kernel may reach another device: no remote copies, remote signals or barrier semaphores. Data moves between devices by JAX's collectives and lax.ppermute only.
A program may use at most 128 MiB of HBM per device.

```python
import jax
import jax.numpy as jnp
from jax import lax

D = 512
VARS = 227
NB = 128
GB_DEV = 24
FAN = 3
PR_DEV = 2
PC_DEV = 2
A = 4
LAYERS = 2
NGB = 3072
NG = 393216
PR = 16
PC = 32
N_GRID = 8
N_MESH = 16


def touch_ends(entries, stream_key, least, top_value):
    spot = [jax.random.randint(jax.random.fold_in(stream_key, axis), (), 0, length) for axis, length in enumerate(entries.shape)]
    widest = entries.shape.index(max(entries.shape))
    neighbour = spot[:widest] + [(spot[widest] + 1) % entries.shape[widest]] + spot[widest + 1:]
    return entries.at[tuple(spot)].set(least).at[tuple(neighbour)].set(top_value)


def steps_of(rng, shape, pieces, least, high):
    def one(dim, parts):
        draws = jax.random.uniform(jax.random.fold_in(jax.random.fold_in(rng, 6), dim), (parts,), jnp.float32, least / len(pieces), high / len(pieces))
        return jnp.repeat(jnp.exp(draws), shape[dim] // parts).reshape((-1,) + (1,) * (len(shape) - dim - 1))

    loudness = one(*pieces[0])
    for cut in pieces[1:]:
        loudness = loudness * one(*cut)
    return loudness


def distinct(rng, rows, count, top, lift):
    sequence = jax.random.permutation(jax.random.fold_in(rng, 1), count)
    pull = sequence
    for power in range(3):
        pull = pull * pull // count
    pull = pull * lift // count
    lots = jax.random.randint(jax.random.fold_in(rng, 2), (rows, count), 0, 4096) + pull
    sure = jax.random.permutation(jax.random.fold_in(rng, 3), rows)[jnp.arange(count) % rows]
    lots = jnp.where(jnp.arange(rows)[:, None] == sure[None, :], 1 << 14, lots)
    priority = lots * count + jnp.arange(count)
    return lax.top_k(priority.astype(jnp.int32), top)[1].astype(jnp.int32)


def centred(key, dims, width, reach, pieces=(), kind=jnp.bfloat16):
    array = jax.random.normal(key, dims, jnp.float32) * width
    if len(pieces) > 0:
        array = steps_of(key, dims, pieces, -0.22, 0.18) * array
    return jnp.clip(array, min=-reach, max=reach).astype(kind)


def setup_inputs(seed: int = 0) -> dict:
    keys = jax.random.split(jax.random.key(seed), 16)
    grid_inputs = centred(keys[0], (NG, VARS), 1.0, 6.0, ((0, 128),))
    embed_weight = centred(keys[1], (VARS, D), VARS ** -0.5, 0.375)
    send_weight = centred(keys[2], (D, D), D ** -0.5, 0.25)
    g2m_dest = distinct(keys[3], NGB, PR_DEV * PC_DEV * N_MESH, FAN, 384)
    g2m_edges = centred(keys[4], (NGB, FAN, NB, NB), (NB * FAN) ** -0.5, 0.3125, ((0, 128),))
    encode_weight = centred(keys[5], (D, D), D ** -0.5, 0.25)
    adj_codes = touch_ends(jax.random.randint(keys[6], (PR, PC, A), 0, 9), jax.random.fold_in(keys[6], 1), 0, 8).astype(jnp.int32)
    adj_count = touch_ends(jax.random.randint(keys[7], (PR, PC), 1, A + 1), jax.random.fold_in(keys[7], 1), 1, A).astype(jnp.int32)
    couplings = centred(keys[8], (PR, PC, A, NB, NB), (NB * A) ** -0.5, 0.25, ((0, 8), (1, 16)))
    message_weight = centred(keys[9], (LAYERS, D, D), D ** -0.5, 0.25)
    node_weight = centred(keys[10], (LAYERS, D, D), D ** -0.5, 0.25)
    decode_weight = centred(keys[11], (D, D), D ** -0.5, 0.25)
    m2g_src = distinct(keys[12], NGB, PR_DEV * PC_DEV * N_MESH, FAN, 384)
    m2g_edges = centred(keys[13], (NGB, FAN, NB, NB), (NB * FAN) ** -0.5, 0.3125, ((0, 128),))
    output_weight = centred(keys[14], (D, VARS), D ** -0.5, 0.25)
    return dict(grid_inputs=grid_inputs, embed_weight=embed_weight, send_weight=send_weight, g2m_dest=g2m_dest, g2m_edges=g2m_edges, encode_weight=encode_weight, adj_codes=adj_codes, adj_count=adj_count, couplings=couplings, message_weight=message_weight, node_weight=node_weight, decode_weight=decode_weight, m2g_src=m2g_src, m2g_edges=m2g_edges, output_weight=output_weight)


epsilon = 1e-05

def reference(grid_inputs, embed_weight, send_weight, g2m_dest, g2m_edges, encode_weight, adj_codes, adj_count, couplings, message_weight, node_weight, decode_weight, m2g_src, m2g_edges, output_weight):
    band_blocks = GB_DEV * N_MESH
    band_patches = PR_DEV * PC
    grid_latent = jax.nn.silu(jnp.dot(grid_inputs, embed_weight, preferred_element_type=jnp.float32)).astype(jnp.bfloat16)
    grid_proj = jnp.dot(grid_latent, send_weight, preferred_element_type=jnp.float32).astype(jnp.bfloat16)
    proj_blocks = grid_proj.reshape(N_GRID, N_MESH, GB_DEV, NB, D)
    enc_edges = g2m_edges.reshape(N_GRID, N_MESH, GB_DEV, FAN, NB, NB)
    dest_codes = g2m_dest.reshape(N_GRID, N_MESH, GB_DEV * FAN).astype(jnp.int32)

    def encode_band(operands):
        blocks_band, edges_band, dest_band = operands

        def add_group(total, group):
            blocks_here, edges_here, dest_here = group
            messages = jnp.einsum('bjmn,bmd->bjnd', edges_here.astype(jnp.float32), blocks_here.astype(jnp.float32))
            partial_sum = jax.ops.segment_sum(messages.reshape(-1, NB, D), dest_here, num_segments=band_patches)
            rounded = partial_sum.astype(jnp.bfloat16).astype(jnp.float32)
            return (total + rounded, None)
        start = jnp.zeros((band_patches, NB, D), jnp.float32)
        total, unused = lax.scan(add_group, start, (blocks_band, edges_band, dest_band))
        return total
    encoded = lax.map(encode_band, (proj_blocks, enc_edges, dest_codes))
    encoded = encoded.reshape(PR * PC * NB, D)
    enc_act = jax.nn.silu(encoded).astype(jnp.bfloat16)
    mesh_state = jnp.dot(enc_act, encode_weight, preferred_element_type=jnp.float32).astype(jnp.bfloat16)
    patch_rows = jnp.arange(PR, dtype=jnp.int32)[:, None, None] + adj_codes // 3
    patch_cols = jnp.arange(PC, dtype=jnp.int32)[None, :, None] + adj_codes % 3
    neighbour_index = (patch_rows * (PC + 2) + patch_cols).astype(jnp.int32)
    live_mask = jnp.arange(A, dtype=jnp.int32)[None, None, :] < adj_count[:, :, None]
    live_couplings = couplings * live_mask[:, :, :, None, None].astype(jnp.bfloat16)
    for layer_index in range(LAYERS):
        sent_state = jnp.dot(mesh_state, message_weight[layer_index], preferred_element_type=jnp.float32).astype(jnp.bfloat16)
        padded = jnp.pad(sent_state.reshape(PR, PC, NB, D), ((1, 1), (1, 1), (0, 0), (0, 0))).reshape(-1, NB, D)

        def one_row(operands):
            index_row, coupling_row = operands
            neighbours = padded[index_row]
            return jnp.einsum('pamn,pamd->pnd', coupling_row.astype(jnp.float32), neighbours.astype(jnp.float32))
        gathered_sum = lax.map(one_row, (neighbour_index, live_couplings))
        activated = jax.nn.silu(gathered_sum.reshape(-1, D))
        normed = (activated * lax.rsqrt(lax.optimization_barrier(jnp.mean(activated * activated, axis=-1, keepdims=True)) + epsilon)).astype(jnp.bfloat16)
        mesh_state = (mesh_state.astype(jnp.float32) + jnp.dot(normed, node_weight[layer_index], preferred_element_type=jnp.float32)).astype(jnp.bfloat16)
    dec_proj = jnp.dot(mesh_state, decode_weight, preferred_element_type=jnp.float32).astype(jnp.bfloat16)
    dec_proj = dec_proj.reshape(N_GRID, band_patches, NB, D)
    dec_edges = m2g_edges.reshape(N_GRID, band_blocks, FAN, NB, NB)
    source_ids = m2g_src.reshape(N_GRID, band_blocks, FAN).astype(jnp.int32)

    def decode_band(operands):
        band_proj, edges_here, source_here = operands
        taken = band_proj[source_here]
        return jnp.einsum('bjmn,bjmd->bnd', edges_here.astype(jnp.float32), taken.astype(jnp.float32))
    decoded = lax.map(decode_band, (dec_proj, dec_edges, source_ids)).reshape(NG, D)
    grid_hidden = jax.nn.silu(decoded).astype(jnp.bfloat16)
    prediction = grid_inputs.astype(jnp.float32) + jnp.dot(grid_hidden, output_weight, preferred_element_type=jnp.float32)
    return prediction.astype(jnp.bfloat16)
```

```python
import functools

import jax
import jax.numpy as jnp
from jax import lax
from jax.experimental import pallas as pl
from jax.experimental.pallas import tpu as pltpu
from jax.sharding import PartitionSpec as P

epsilon = 1e-05
BF16 = jnp.bfloat16
F32 = jnp.float32
SIDE = 4
NB = 128
D = 512
HALF = 256
OWN = 4
PARAMS = pltpu.CompilerParams(vmem_limit_bytes=56 * 1024 * 1024)


def dot(a, b):
    return jnp.dot(a, b, preferred_element_type=F32)


def dot_t(a, b):
    return lax.dot_general(a, b, (((0,), (0,)), ((), ())), preferred_element_type=F32)


def silu(v):
    return v * jax.nn.sigmoid(v)


def shift(value, axis, step):
    pairs = []
    for y in range(SIDE):
        for z in range(SIDE):
            to = ((y + step) % SIDE, z) if axis == 0 else (y, (z + step) % SIDE)
            pairs.append((y * SIDE + z, to[0] * SIDE + to[1]))
    return lax.ppermute(value, "mesh", pairs)


class Links:
    def __init__(self):
        self.last = {}

    def send(self, value, axis, step):
        link = (axis, step)
        if link in self.last:
            value, _ = lax.optimization_barrier((value, self.last[link]))
        self.last[link] = shift(value, axis, step)
        return self.last[link]


def place(code):
    row = code // 32
    col = code % 32
    owner = col // 2
    return owner // SIDE, owner % SIDE, row * 2 + col % 2


PARTS = ((2, 1), (3, 0))
ORDER = ((2, 0), (3, 0), (2, 1), (1, 0), (3, 1), (1, 1), (0, 0), (0, 1))
BLOCKS = 4
STEPS = 6


def encode_kernel(dest_ref, x_ref, embed_ref, send_ref, edges_ref, *rest):
    outs, (acc, stage, sems) = rest[:16], rest[16:]
    i = pl.program_id(0)

    @pl.when(i == 0)
    def _():
        acc[...] = jnp.zeros_like(acc)

    latent = silu(dot_t(x_ref[...], embed_ref[...])).astype(BF16)
    proj = dot(latent, send_ref[...]).astype(BF16)
    me = lax.axis_index("mesh")
    my_y, my_z = me // SIDE, me % SIDE
    for b in range(BLOCKS):
        block = proj[b * NB : (b + 1) * NB]
        for j in range(3):
            y, z, local = place(dest_ref[j, i * BLOCKS + b])
            slot = (((y - my_y) & 3) * SIDE + ((z - my_z) & 3)) * OWN + local
            acc[slot] += dot_t(edges_ref[b, j], block)

    @pl.when(i == STEPS - 1)
    def _():
        copies = []
        for n, (k, part) in enumerate(ORDER):
            for h in range(2):
                for m, q in enumerate(PARTS[part]):
                    base = (k * SIDE + q if h == 0 else q * SIDE + k) * OWN
                    stage[h, n, m * OWN : (m + 1) * OWN] = acc[
                        base : base + OWN, :, h * HALF : (h + 1) * HALF
                    ].astype(BF16)
                copy = pltpu.make_async_copy(stage.at[h, n], outs[h * 8 + n], sems.at[h * 8 + n])
                copy.start()
                copies.append(copy)
        for copy in copies:
            copy.wait()


def encode(grid_inputs, embed_weight, send_weight, g2m_dest, g2m_edges):
    rows = BLOCKS * NB

    inputs_t = grid_inputs.T
    return pl.pallas_call(
        encode_kernel,
        grid_spec=pltpu.PrefetchScalarGridSpec(
            num_scalar_prefetch=1,
            grid=(STEPS,),
            in_specs=[
                pl.BlockSpec((inputs_t.shape[0], rows), lambda i, *_: (0, i)),
                pl.BlockSpec(embed_weight.shape, lambda i, *_: (0, 0)),
                pl.BlockSpec(send_weight.shape, lambda i, *_: (0, 0)),
                pl.BlockSpec((BLOCKS, 3, NB, NB), lambda i, *_: (i, 0, 0, 0)),
            ],
            out_specs=[pl.BlockSpec(memory_space=pl.ANY)] * 16,
            scratch_shapes=[
                pltpu.VMEM((64, NB, D), F32),
                pltpu.VMEM((2, 8, 8, NB, HALF), BF16),
                pltpu.SemaphoreType.DMA((16,)),
            ],
        ),
        out_shape=[jax.ShapeDtypeStruct((8, NB, HALF), BF16)] * 16,
        compiler_params=PARAMS,
        name="encode",
    )(g2m_dest.T, inputs_t, embed_weight, send_weight, g2m_edges)


def add(*values):
    total = values[0].astype(F32)
    for value in values[1:]:
        total = total + value.astype(F32)
    return total.astype(BF16)


def reduce(pieces):
    both = range(2)
    links = Links()
    piece = [dict(zip(ORDER, pieces[8 * h : 8 * h + 8])) for h in both]

    def far(part, step):
        return [links.send(piece[h][2, part], h, step) for h in both]

    def near(part, step, got):
        k = step % SIDE
        sent = []
        for h in both:
            value = piece[h][k, part]
            sent.append(links.send(value if got is None else add(value, got[h]), h, step))
        return sent

    def settled(part, at, up, down, *more):
        rows = slice(at * OWN, (at + 1) * OWN)
        values = [piece[h][0, part][rows] for h in both]
        return [
            add(values[h], up[h][rows], down[h][rows], *[m[h] for m in more]) for h in both
        ]

    far_0 = far(0, 1)
    down_0 = near(0, -1, None)
    up_0 = near(0, 1, far_0)
    far_1 = far(1, -1)
    sums_2 = settled(0, 0, up_0, down_0)
    from_2 = [links.send(sums_2[h], 1 - h, 1) for h in both]
    down_1 = near(1, -1, far_1)
    up_1 = near(1, 1, None)
    sums_1 = settled(0, 1, up_0, down_0, from_2)
    from_1 = [links.send(sums_1[h], 1 - h, 1) for h in both]
    sums_3 = settled(1, 0, up_1, down_1)
    from_3 = [links.send(sums_3[h], 1 - h, -1) for h in both]
    terms = []
    for h in both:
        terms += [piece[h][0, 1], up_1[h], down_1[h], from_1[h], from_3[h]]
    return terms


def start_kernel(*refs):
    terms, (encode_ref, message_ref, mesh_ref, *sent_refs) = refs[:10], refs[10:]
    total = None
    for h in range(2):
        value = None
        for term in terms[5 * h : 5 * h + 5]:
            term = term[term.shape[0] - OWN :].astype(F32)
            value = term if value is None else value + term
        act = silu(value).astype(BF16).reshape(OWN * NB, HALF)
        part = dot(act, encode_ref[h * HALF : (h + 1) * HALF, :])
        total = part if total is None else total + part
    mesh = total.astype(BF16)
    mesh_ref[...] = mesh
    put_sent(dot(mesh, message_ref[0]).astype(BF16), sent_refs)


def put_sent(sent, refs):
    sent = sent.reshape(2, 2, NB, D)
    all_ref, first_ref, last_ref = refs
    all_ref[...] = sent
    first_ref[...] = sent[:, 0]
    last_ref[...] = sent[:, 1]


def sent_shapes():
    column = jax.ShapeDtypeStruct((2, NB, D), BF16)
    return [
        jax.ShapeDtypeStruct((OWN * NB, D), BF16),
        jax.ShapeDtypeStruct((2, 2, NB, D), BF16),
        column,
        column,
    ]


def mesh_start(terms, encode_weight, message_weight):
    return pl.pallas_call(
        start_kernel,
        out_shape=sent_shapes(),
        compiler_params=PARAMS,
        name="mesh_start",
    )(*terms, encode_weight, message_weight)


def step_kernel(layer, codes_ref, count_ref, mesh_ref, own_ref, left_ref, right_ref, above_ref, below_ref,
                couplings_ref, node_ref, next_ref, *rest):
    outs, (pad, normed) = rest[:-2], rest[-2:]
    pad[0:4] = above_ref[...]
    pad[12:16] = below_ref[...]
    for r in range(2):
        pad[4 * (r + 1)] = left_ref[r]
        pad[4 * (r + 1) + 1 : 4 * (r + 1) + 3] = own_ref[r]
        pad[4 * (r + 1) + 3] = right_ref[r]
    for r in range(2):
        for c in range(2):
            near, weights = [], []
            for a in range(4):
                code = codes_ref[r * 2 + c, a]
                near.append(pad[(r + code // 3) * 4 + c + code % 3])
                live = (a < count_ref[r, c]).astype(BF16)
                weights.append(couplings_ref[r, c, a] * live)
            agg = dot_t(jnp.concatenate(weights, 0), jnp.concatenate(near, 0))
            act = silu(agg)
            scale = lax.rsqrt(jnp.mean(act * act, axis=-1, keepdims=True) + epsilon)
            at = (r * 2 + c) * NB
            normed[at : at + NB, :] = (act * scale).astype(BF16)
    mesh = (mesh_ref[...].astype(F32) + dot(normed[...], node_ref[layer])).astype(BF16)
    if layer == 0:
        outs[0][...] = mesh
        put_sent(dot(mesh, next_ref[1]).astype(BF16), outs[1:])
    else:
        proj = dot(mesh, next_ref[...]).astype(BF16).reshape(OWN, NB, D)
        outs[0][...] = proj[:, :, :HALF]
        outs[1][...] = proj[:, :, HALF:]


def mesh_step(layer, codes, count, mesh, sent, halo, couplings, node_weight, next_weight):
    if layer == 0:
        out_shape = sent_shapes()
    else:
        out_shape = [jax.ShapeDtypeStruct((OWN, NB, HALF), BF16)] * 2
    smem = pl.BlockSpec(memory_space=pltpu.SMEM)
    vmem = pl.BlockSpec(memory_space=pltpu.VMEM)
    return pl.pallas_call(
        functools.partial(step_kernel, layer),
        in_specs=[smem, smem] + [vmem] * 9,
        out_shape=out_shape,
        scratch_shapes=[pltpu.VMEM((16, NB, D), BF16), pltpu.VMEM((OWN * NB, D), BF16)],
        compiler_params=PARAMS,
        name="mesh_step",
    )(codes, count, mesh, sent[0], *halo, couplings, node_weight, next_weight)


def halo_of(grid, first, last):
    size, length = lax.axis_size("mesh"), lax.axis_size("grid")
    ahead = lambda n: [(i, i + 1) for i in range(n - 1)]
    back = lambda n: [(i + 1, i) for i in range(n - 1)]
    left = lax.ppermute(last, "mesh", ahead(size))
    right = lax.ppermute(first, "mesh", back(size))
    top = jnp.concatenate([left[:1], grid[0], right[:1]], 0)
    bottom = jnp.concatenate([left[1:], grid[1], right[1:]], 0)
    above = lax.ppermute(bottom, "grid", ahead(length))
    below = lax.ppermute(top, "grid", back(length))
    return left, right, above, below


def gather(owns):
    both = range(2)
    links = Links()
    near_1 = [links.send(owns[h], 1 - h, 1) for h in both]
    near_3 = [links.send(owns[h], 1 - h, -1) for h in both]
    part_0 = [jnp.concatenate([owns[h], near_1[h]], 0) for h in both]
    near_2 = [links.send(near_1[h], 1 - h, 1) for h in both]
    down_0 = [links.send(part_0[h], h, -1) for h in both]
    up_0 = [links.send(part_0[h], h, 1) for h in both]
    part_1 = [jnp.concatenate([near_2[h], near_3[h]], 0) for h in both]
    down_1 = [links.send(part_1[h], h, -1) for h in both]
    up_1 = [links.send(part_1[h], h, 1) for h in both]
    far_0 = [links.send(up_0[h], h, 1) for h in both]
    far_1 = [links.send(down_1[h], h, -1) for h in both]
    held = []
    for h in both:
        held += [part_0[h], part_1[h], up_0[h], up_1[h], far_0[h], far_1[h], down_0[h], down_1[h]]
    return held


def decode_kernel(src_ref, x_ref, edges_ref, output_ref, *rest):
    pieces, (out_ref, held, sems) = rest[:16], rest[16:]
    i = pl.program_id(0)

    @pl.when(i == 0)
    def _():
        copies = []
        for n in range(16):
            copy = pltpu.make_async_copy(
                pieces[n], held.at[n // 8, pl.ds(n % 8 * 8, 8)], sems.at[n]
            )
            copy.start()
            copies.append(copy)
        for copy in copies:
            copy.wait()

    me = lax.axis_index("mesh")
    my_y, my_z = me // SIDE, me % SIDE
    for b in range(BLOCKS):
        first, second = [], []
        for j in range(3):
            y, z, local = place(src_ref[j, i * BLOCKS + b])
            ky, kz = (my_y - y) & 3, (my_z - z) & 3
            first.append(held[0, (ky * SIDE + kz) * OWN + local])
            second.append(held[1, (kz * SIDE + ky) * OWN + local])
        edges = edges_ref[b].reshape(3 * NB, NB)
        total = None
        for h, parts in enumerate((first, second)):
            hidden = silu(dot_t(edges, jnp.concatenate(parts, 0))).astype(BF16)
            term = lax.dot_general(
                output_ref[:, h * HALF : (h + 1) * HALF],
                hidden,
                (((1,), (1,)), ((), ())),
                preferred_element_type=F32,
            )
            total = term if total is None else total + term
        columns = pl.ds(b * NB, NB)
        out_ref[:, columns] = (x_ref[:, columns].astype(F32) + total).astype(BF16)


def decode(grid_inputs, m2g_src, m2g_edges, output_weight, pieces):
    rows = BLOCKS * NB
    inputs_t, output_t = grid_inputs.T, output_weight.T
    width = inputs_t.shape[0]
    result = pl.pallas_call(
        decode_kernel,
        grid_spec=pltpu.PrefetchScalarGridSpec(
            num_scalar_prefetch=1,
            grid=(STEPS,),
            in_specs=[
                pl.BlockSpec((width, rows), lambda i, *_: (0, i)),
                pl.BlockSpec((BLOCKS, 3, NB, NB), lambda i, *_: (i, 0, 0, 0)),
                pl.BlockSpec(output_t.shape, lambda i, *_: (0, 0)),
            ]
            + [pl.BlockSpec(memory_space=pl.ANY)] * 16,
            out_specs=pl.BlockSpec((width, rows), lambda i, *_: (0, i)),
            scratch_shapes=[
                pltpu.VMEM((2, 64, NB, HALF), BF16),
                pltpu.SemaphoreType.DMA((16,)),
            ],
        ),
        out_shape=jax.ShapeDtypeStruct(inputs_t.shape, BF16),
        compiler_params=PARAMS,
        name="decode",
    )(m2g_src.T, inputs_t, m2g_edges, output_t, *pieces)
    return result.T


def per_device(
    grid_inputs,
    embed_weight,
    send_weight,
    g2m_dest,
    g2m_edges,
    encode_weight,
    adj_codes,
    adj_count,
    couplings,
    message_weight,
    node_weight,
    decode_weight,
    m2g_src,
    m2g_edges,
    output_weight,
):
    pieces = encode(grid_inputs, embed_weight, send_weight, g2m_dest, g2m_edges)
    mesh, *sent = mesh_start(reduce(pieces), encode_weight, message_weight)
    codes = adj_codes.reshape(OWN, -1)
    mesh, *sent = mesh_step(
        0, codes, adj_count, mesh, sent, halo_of(*sent), couplings, node_weight, message_weight
    )
    owns = mesh_step(
        1, codes, adj_count, mesh, sent, halo_of(*sent), couplings, node_weight, decode_weight
    )
    return decode(grid_inputs, m2g_src, m2g_edges, output_weight, gather(owns))


def solution(mesh):
    placed = (
        P(("grid", "mesh"), None),
        P(),
        P(),
        P(("grid", "mesh"), None),
        P(("grid", "mesh"), None, None, None),
        P(),
        P("grid", "mesh", None),
        P("grid", "mesh"),
        P("grid", "mesh", None, None, None),
        P(),
        P(),
        P(),
        P(("grid", "mesh"), None),
        P(("grid", "mesh"), None, None, None),
        P(),
    )
    return jax.shard_map(
        per_device, mesh=mesh, in_specs=placed, out_specs=P(("grid", "mesh"), None), check_vma=False
    )
```

```python
import functools

import jax
import jax.numpy as jnp
from jax import lax
from jax.experimental import pallas as pl
from jax.experimental.pallas import tpu as pltpu
from jax.sharding import PartitionSpec as P

epsilon = 1e-05
BF16 = jnp.bfloat16
F32 = jnp.float32
SIDE = 4
NB = 128
D = 512
HALF = 256
OWN = 4


def params(mib):
    return pltpu.CompilerParams(vmem_limit_bytes=mib * 1024 * 1024)


def dot(a, b):
    return jnp.dot(a, b, preferred_element_type=F32)


def dot_t(a, b):
    return lax.dot_general(a, b, (((0,), (0,)), ((), ())), preferred_element_type=F32)


def silu(v):
    half = 0.5 * v
    return half + half * jnp.tanh(half)


def shift(value, axis, step):
    pairs = []
    for y in range(SIDE):
        for z in range(SIDE):
            to = ((y + step) % SIDE, z) if axis == 0 else (y, (z + step) % SIDE)
            pairs.append((y * SIDE + z, to[0] * SIDE + to[1]))
    return lax.ppermute(value, "mesh", pairs)


class Links:
    def __init__(self):
        self.last = {}

    def send(self, value, axis, step):
        link = (axis, step)
        if link in self.last:
            value, _ = lax.optimization_barrier((value, self.last[link]))
        self.last[link] = shift(value, axis, step)
        return self.last[link]


def place(code):
    row = code // 32
    col = code % 32
    owner = col // 2
    return owner // SIDE, owner % SIDE, row * 2 + col % 2


CHUNKS = 3
CHUNK_BLOCKS = 8
CHUNK = CHUNK_BLOCKS * NB


def encode_kernel(dest_ref, x_hbm, embed_hbm, send_hbm, edges_hbm, out_0, out_1, x, embed, send, edges, sems):
    copies = [
        pltpu.make_async_copy(embed_hbm, embed, sems.at[0]),
        pltpu.make_async_copy(x_hbm.at[:, pl.ds(0, CHUNK)], x.at[0], sems.at[1]),
        pltpu.make_async_copy(send_hbm, send, sems.at[2]),
        pltpu.make_async_copy(edges_hbm.at[pl.ds(0, CHUNK_BLOCKS)], edges.at[0], sems.at[3]),
    ]
    for c in range(1, CHUNKS):
        copies += [
            pltpu.make_async_copy(x_hbm.at[:, pl.ds(c * CHUNK, CHUNK)], x.at[c], sems.at[2 * c + 2]),
            pltpu.make_async_copy(
                edges_hbm.at[pl.ds(c * CHUNK_BLOCKS, CHUNK_BLOCKS)], edges.at[c], sems.at[2 * c + 3]
            ),
        ]
    for copy in copies:
        copy.start()
    out_0[...] = jnp.zeros_like(out_0)
    out_1[...] = jnp.zeros_like(out_1)
    me = lax.axis_index("mesh")
    my_y, my_z = me // SIDE, me % SIDE
    for c in range(CHUNKS):
        if c == 0:
            copies[0].wait()
            copies[1].wait()
        else:
            copies[2 * c + 2].wait()
        latent = silu(dot_t(x[c], embed[...])).astype(BF16)
        if c == 0:
            copies[2].wait()
        proj = dot(latent, send[...]).astype(BF16)
        copies[2 * c + 3].wait()
        for b in range(CHUNK_BLOCKS):
            weights = jnp.concatenate([edges[c, b, j] for j in range(3)], 1)
            message = dot_t(weights, proj[b * NB : (b + 1) * NB])
            for j in range(3):
                y, z, local = place(dest_ref[j, c * CHUNK_BLOCKS + b])
                dy, dz = (y - my_y) & 3, (z - my_z) & 3
                part = message[j * NB : (j + 1) * NB]
                at_0 = (dy * SIDE + ((2 - dz) & 3)) * OWN + local
                at_1 = (dz * SIDE + ((2 - dy) & 3)) * OWN + local
                out_0[at_0] = (out_0[at_0].astype(F32) + part[:, :HALF]).astype(BF16)
                out_1[at_1] = (out_1[at_1].astype(F32) + part[:, HALF:]).astype(BF16)


def in_hbm(value):
    return pltpu.with_memory_space_constraint(value, pltpu.HBM)


def encode(grid_inputs, embed_weight, send_weight, g2m_dest, g2m_edges):
    inputs_t = grid_inputs.T
    width = inputs_t.shape[0]
    halves = pl.pallas_call(
        encode_kernel,
        in_specs=[pl.BlockSpec(memory_space=pltpu.SMEM)] + [pl.BlockSpec(memory_space=pltpu.HBM)] * 4,
        out_specs=[pl.BlockSpec(memory_space=pltpu.VMEM)] * 2,
        out_shape=[pltpu.VMEM((64, NB, HALF), BF16)] * 2,
        scratch_shapes=[
            pltpu.VMEM((CHUNKS, width, CHUNK), BF16),
            pltpu.VMEM(embed_weight.shape, BF16),
            pltpu.VMEM(send_weight.shape, BF16),
            pltpu.VMEM((CHUNKS, CHUNK_BLOCKS, 3, NB, NB), BF16),
            pltpu.SemaphoreType.DMA((2 * CHUNKS + 2,)),
        ],
        compiler_params=params(28),
        name="encode",
    )(*map(in_hbm, (g2m_dest.T, inputs_t, embed_weight, send_weight, g2m_edges)))
    cuts = [(k, part) for k in range(4) for part in range(2)]
    return [
        dict(zip(cuts, lax.optimization_barrier([half[16 * k + 8 * part :][:8] for k, part in cuts])))
        for half in halves
    ]


def add(*values):
    total = values[0].astype(F32)
    for value in values[1:]:
        total = total + value.astype(F32)
    return total.astype(BF16)


def reduce(piece):
    both = range(2)
    links = Links()

    def far(part, step):
        return [links.send(piece[h][2, part], h, step) for h in both]

    def near(part, step, got):
        k = step % SIDE
        sent = []
        for h in both:
            value = piece[h][k, part]
            sent.append(links.send(value if got is None else add(value, got[h]), h, step))
        return sent

    def settled(part, at, up, down, *more):
        rows = slice(at * OWN, (at + 1) * OWN)
        values = [piece[h][0, part][rows] for h in both]
        return [
            add(values[h], up[h][rows], down[h][rows], *[m[h] for m in more]) for h in both
        ]

    far_0 = far(0, 1)
    down_0 = near(0, -1, None)
    up_0 = near(0, 1, far_0)
    far_1 = far(1, -1)
    sums_2 = settled(0, 0, up_0, down_0)
    from_2 = [links.send(sums_2[h], 1 - h, 1) for h in both]
    down_1 = near(1, -1, far_1)
    up_1 = near(1, 1, None)
    sums_1 = settled(0, 1, up_0, down_0, from_2)
    from_1 = [links.send(sums_1[h], 1 - h, 1) for h in both]
    sums_3 = settled(1, 1, up_1, down_1)
    from_3 = [links.send(sums_3[h], 1 - h, -1) for h in both]
    terms = []
    for h in both:
        terms += [piece[h][0, 1], up_1[h], down_1[h], from_1[h], from_3[h]]
    return terms


def start_kernel(*refs):
    terms, (encode_ref, message_ref, mesh_ref, *sent_refs) = refs[:10], refs[10:]
    total = None
    for h in range(2):
        value = None
        for term in terms[5 * h : 5 * h + 5]:
            term = term[:OWN].astype(F32)
            value = term if value is None else value + term
        act = silu(value).astype(BF16).reshape(OWN * NB, HALF)
        part = dot(act, encode_ref[h * HALF : (h + 1) * HALF, :])
        total = part if total is None else total + part
    mesh = total.astype(BF16)
    mesh_ref[...] = mesh
    put_sent(dot(mesh, message_ref[0]).astype(BF16), sent_refs)


def put_sent(sent, refs):
    sent = sent.reshape(2, 2, NB, D)
    for n in range(2):
        refs[n][...] = sent[n]
        refs[2 + n][...] = sent[:, n]


def sent_shapes():
    return [jax.ShapeDtypeStruct((OWN * NB, D), BF16)] + [
        jax.ShapeDtypeStruct((2, NB, D), BF16)
    ] * 4


def mesh_start(terms, encode_weight, message_weight):
    return pl.pallas_call(
        start_kernel,
        out_shape=sent_shapes(),
        compiler_params=params(12),
        name="mesh_start",
    )(*terms, encode_weight, message_weight)


def step_kernel(layer, codes_ref, count_ref, mesh_ref, *rest):
    band, (couplings_ref, node_ref, next_ref), rest = rest[:8], rest[8:11], rest[11:]
    outs, (pad, normed) = rest[:-2], rest[-2:]
    left, right, above, rows_0, rows_1, below, corners_above, corners_below = band
    for row, middle in enumerate((above, rows_0, rows_1, below)):
        pad[4 * row + 1 : 4 * row + 3] = middle[...]
    for r in range(2):
        pad[4 * r + 4] = left[r]
        pad[4 * r + 7] = right[r]
        pad[3 * r] = corners_above[r]
        pad[12 + 3 * r] = corners_below[r]
    for r in range(2):
        for c in range(2):
            near, weights = [], []
            for a in range(4):
                code = codes_ref[r * 2 + c, a]
                near.append(pad[(r + code // 3) * 4 + c + code % 3])
                live = (a < count_ref[r, c]).astype(BF16)
                weights.append(couplings_ref[r, c, a] * live)
            agg = dot_t(jnp.concatenate(weights, 0), jnp.concatenate(near, 0))
            act = silu(agg)
            scale = lax.rsqrt(jnp.mean(act * act, axis=-1, keepdims=True) + epsilon)
            at = (r * 2 + c) * NB
            normed[at : at + NB, :] = (act * scale).astype(BF16)
    mesh = (mesh_ref[...].astype(F32) + dot(normed[...], node_ref[layer])).astype(BF16)
    if layer == 0:
        outs[0][...] = mesh
        put_sent(dot(mesh, next_ref[1]).astype(BF16), outs[1:])
    else:
        proj = dot(mesh, next_ref[...]).astype(BF16).reshape(OWN, NB, D)
        outs[0][...] = proj[:, :, :HALF]
        outs[1][...] = proj[:, :, HALF:]


def mesh_step(layer, codes, count, mesh, band, couplings, node_weight, next_weight):
    if layer == 0:
        out_shape = sent_shapes()
    else:
        out_shape = [jax.ShapeDtypeStruct((OWN, NB, HALF), BF16)] * 2
    smem = pl.BlockSpec(memory_space=pltpu.SMEM)
    vmem = pl.BlockSpec(memory_space=pltpu.VMEM)
    return pl.pallas_call(
        functools.partial(step_kernel, layer),
        in_specs=[smem, smem] + [vmem] * 12,
        out_shape=out_shape,
        scratch_shapes=[pltpu.VMEM((16, NB, D), BF16), pltpu.VMEM((OWN * NB, D), BF16)],
        compiler_params=params(16),
        name="mesh_step",
    )(codes, count, mesh, *band, couplings, node_weight, next_weight)


def band_of(row_0, row_1, first, last):
    size, length = lax.axis_size("mesh"), lax.axis_size("grid")
    ahead = lambda n: [(i, i + 1) for i in range(n - 1)]
    back = lambda n: [(i + 1, i) for i in range(n - 1)]
    left = lax.ppermute(last, "mesh", ahead(size))
    right = lax.ppermute(first, "mesh", back(size))
    above = lax.ppermute(row_1, "grid", ahead(length))
    below = lax.ppermute(row_0, "grid", back(length))
    corners = [jnp.concatenate([left[r : r + 1], right[r : r + 1]], 0) for r in range(2)]
    corners_above = lax.ppermute(corners[1], "grid", ahead(length))
    corners_below = lax.ppermute(corners[0], "grid", back(length))
    return left, right, above, row_0, row_1, below, corners_above, corners_below


BLOCKS = 8
STEPS = 3


def gather(owns):
    both = range(2)
    links = Links()
    near_1 = [links.send(owns[h], 1 - h, 1) for h in both]
    near_3 = [links.send(owns[h], 1 - h, -1) for h in both]
    part_0 = [jnp.concatenate([owns[h], near_1[h]], 0) for h in both]
    near_2 = [links.send(near_1[h], 1 - h, 1) for h in both]
    down_0 = [links.send(part_0[h], h, -1) for h in both]
    up_0 = [links.send(part_0[h], h, 1) for h in both]
    part_1 = [jnp.concatenate([near_2[h], near_3[h]], 0) for h in both]
    down_1 = [links.send(part_1[h], h, -1) for h in both]
    up_1 = [links.send(part_1[h], h, 1) for h in both]
    far_0 = [links.send(up_0[h], h, 1) for h in both]
    far_1 = [links.send(down_1[h], h, -1) for h in both]
    held = []
    for h in both:
        held += [part_0[h], part_1[h], up_0[h], up_1[h], far_0[h], far_1[h], down_0[h], down_1[h]]
    return held


def decode_kernel(src_ref, x_ref, edges_ref, output_ref, *rest):
    pieces, (out_ref, held, hidden, sems) = rest[:16], rest[16:]
    i = pl.program_id(0)

    @pl.when(i == 0)
    def _():
        copies = []
        for n in range(16):
            copy = pltpu.make_async_copy(
                pieces[n], held.at[n // 8, pl.ds(n % 8 * 8, 8)], sems.at[n]
            )
            copy.start()
            copies.append(copy)
        for copy in copies:
            copy.wait()

    me = lax.axis_index("mesh")
    my_y, my_z = me // SIDE, me % SIDE
    for b in range(BLOCKS):
        first, second = [], []
        for j in range(3):
            y, z, local = place(src_ref[j, i * BLOCKS + b])
            ky, kz = (my_y - y) & 3, (my_z - z) & 3
            first.append(held[0, (ky * SIDE + kz) * OWN + local])
            second.append(held[1, (kz * SIDE + ky) * OWN + local])
        edges = edges_ref[b].reshape(3 * NB, NB)
        for h, parts in enumerate((first, second)):
            decoded = dot_t(edges, jnp.concatenate(parts, 0))
            hidden[b * NB : (b + 1) * NB, h * HALF : (h + 1) * HALF] = silu(decoded).astype(BF16)
    total = lax.dot_general(
        output_ref[...], hidden[...], (((1,), (1,)), ((), ())), preferred_element_type=F32
    )
    out_ref[...] = (x_ref[...].astype(F32) + total).astype(BF16)


def decode(grid_inputs, m2g_src, m2g_edges, output_weight, pieces):
    rows = BLOCKS * NB
    inputs_t, output_t = grid_inputs.T, output_weight.T
    width = inputs_t.shape[0]
    result = pl.pallas_call(
        decode_kernel,
        grid_spec=pltpu.PrefetchScalarGridSpec(
            num_scalar_prefetch=1,
            grid=(STEPS,),
            in_specs=[
                pl.BlockSpec((width, rows), lambda i, *_: (0, i)),
                pl.BlockSpec((BLOCKS, 3, NB, NB), lambda i, *_: (i, 0, 0, 0)),
                pl.BlockSpec(output_t.shape, lambda i, *_: (0, 0)),
            ]
            + [pl.BlockSpec(memory_space=pl.ANY)] * 16,
            out_specs=pl.BlockSpec((width, rows), lambda i, *_: (0, i)),
            scratch_shapes=[
                pltpu.VMEM((2, 64, NB, HALF), BF16),
                pltpu.VMEM((rows, D), BF16),
                pltpu.SemaphoreType.DMA((16,)),
            ],
        ),
        out_shape=jax.ShapeDtypeStruct(inputs_t.shape, BF16),
        compiler_params=params(20),
        name="decode",
    )(m2g_src.T, inputs_t, m2g_edges, output_t, *pieces)
    return result.T


def per_device(
    grid_inputs,
    embed_weight,
    send_weight,
    g2m_dest,
    g2m_edges,
    encode_weight,
    adj_codes,
    adj_count,
    couplings,
    message_weight,
    node_weight,
    decode_weight,
    m2g_src,
    m2g_edges,
    output_weight,
):
    pieces = encode(grid_inputs, embed_weight, send_weight, g2m_dest, g2m_edges)
    mesh, *sent = mesh_start(reduce(pieces), encode_weight, message_weight)
    codes = adj_codes.reshape(OWN, -1)
    mesh, *sent = mesh_step(
        0, codes, adj_count, mesh, band_of(*sent), couplings, node_weight, message_weight
    )
    owns = mesh_step(
        1, codes, adj_count, mesh, band_of(*sent), couplings, node_weight, decode_weight
    )
    return decode(grid_inputs, m2g_src, m2g_edges, output_weight, gather(owns))


def solution(mesh):
    placed = (
        P(("grid", "mesh"), None),
        P(),
        P(),
        P(("grid", "mesh"), None),
        P(("grid", "mesh"), None, None, None),
        P(),
        P("grid", "mesh", None),
        P("grid", "mesh"),
        P("grid", "mesh", None, None, None),
        P(),
        P(),
        P(),
        P(("grid", "mesh"), None),
        P(("grid", "mesh"), None, None, None),
        P(),
    )
    return jax.shard_map(
        per_device, mesh=mesh, in_specs=placed, out_specs=P(("grid", "mesh"), None), check_vma=False
    )
```

```python
import functools

import jax
import jax.numpy as jnp
from jax import lax
from jax.experimental import pallas as pl
from jax.experimental.pallas import tpu as pltpu
from jax.sharding import PartitionSpec as P

epsilon = 1e-05
BF16 = jnp.bfloat16
F32 = jnp.float32
SIDE = 4
NB = 128
D = 512
HALF = 256
OWN = 4


def params(mib):
    return pltpu.CompilerParams(vmem_limit_bytes=mib * 1024 * 1024)


def dot(a, b):
    return jnp.dot(a, b, preferred_element_type=F32)


def dot_t(a, b):
    return lax.dot_general(a, b, (((0,), (0,)), ((), ())), preferred_element_type=F32)


def silu(v):
    half = 0.5 * v
    return half + half * jnp.tanh(half)


def shift(value, axis, step):
    pairs = []
    for y in range(SIDE):
        for z in range(SIDE):
            to = ((y + step) % SIDE, z) if axis == 0 else (y, (z + step) % SIDE)
            pairs.append((y * SIDE + z, to[0] * SIDE + to[1]))
    return lax.ppermute(value, "mesh", pairs)


class Links:
    def __init__(self):
        self.last = {}

    def send(self, value, axis, step):
        link = (axis, step)
        if link in self.last:
            value, _ = lax.optimization_barrier((value, self.last[link]))
        self.last[link] = shift(value, axis, step)
        return self.last[link]


def place(code):
    row = code // 32
    col = code % 32
    owner = col // 2
    return owner // SIDE, owner % SIDE, row * 2 + col % 2


CHUNKS = 3
CHUNK_BLOCKS = 8
CHUNK = CHUNK_BLOCKS * NB


def encode_kernel(dest_ref, x_hbm, embed_hbm, send_hbm, edges_hbm, out_0, out_1, x, embed, send, edges, sems):
    def inputs(c):
        return (
            pltpu.make_async_copy(
                x_hbm.at[:, pl.ds(pl.multiple_of(c * CHUNK, CHUNK), CHUNK)], x.at[c], sems.at[2 * c + 2]
            ),
            pltpu.make_async_copy(
                edges_hbm.at[pl.ds(c * CHUNK_BLOCKS, CHUNK_BLOCKS)], edges.at[c], sems.at[2 * c + 3]
            ),
        )

    weights = (
        pltpu.make_async_copy(embed_hbm, embed, sems.at[0]),
        pltpu.make_async_copy(send_hbm, send, sems.at[1]),
    )
    for copy in weights + inputs(0):
        copy.start()

    @pl.loop(1, CHUNKS)
    def _(c):
        for copy in inputs(c):
            copy.start()

    @pl.loop(0, 64)
    def _(n):
        out_0[n] = jnp.zeros((NB, HALF), BF16)
        out_1[n] = jnp.zeros((NB, HALF), BF16)

    me = lax.axis_index("mesh")
    my_y, my_z = me // SIDE, me % SIDE
    for copy in weights:
        copy.wait()

    @pl.loop(0, CHUNKS)
    def _(c):
        for copy in inputs(c):
            copy.wait()
        latent = silu(dot_t(x[c], embed[...])).astype(BF16)
        proj = dot(latent, send[...]).astype(BF16)
        for b in range(CHUNK_BLOCKS):
            both = jnp.concatenate([edges[c, b, j] for j in range(3)], 1)
            message = dot_t(both, proj[b * NB : (b + 1) * NB])
            for j in range(3):
                y, z, local = place(dest_ref[j, c * CHUNK_BLOCKS + b])
                dy, dz = (y - my_y) & 3, (z - my_z) & 3
                part = message[j * NB : (j + 1) * NB]
                at_0 = (dy * SIDE + ((2 - dz) & 3)) * OWN + local
                at_1 = (dz * SIDE + ((2 - dy) & 3)) * OWN + local
                out_0[at_0] = (out_0[at_0].astype(F32) + part[:, :HALF]).astype(BF16)
                out_1[at_1] = (out_1[at_1].astype(F32) + part[:, HALF:]).astype(BF16)


def in_hbm(value):
    return pltpu.with_memory_space_constraint(value, pltpu.HBM)


def encode(grid_inputs, embed_weight, send_weight, g2m_dest, g2m_edges):
    inputs_t = grid_inputs.T
    width = inputs_t.shape[0]
    halves = pl.pallas_call(
        encode_kernel,
        in_specs=[pl.BlockSpec(memory_space=pltpu.SMEM)] + [pl.BlockSpec(memory_space=pltpu.HBM)] * 4,
        out_specs=[pl.BlockSpec(memory_space=pltpu.VMEM)] * 2,
        out_shape=[pltpu.VMEM((64, NB, HALF), BF16)] * 2,
        scratch_shapes=[
            pltpu.VMEM((CHUNKS, width, CHUNK), BF16),
            pltpu.VMEM(embed_weight.shape, BF16),
            pltpu.VMEM(send_weight.shape, BF16),
            pltpu.VMEM((CHUNKS, CHUNK_BLOCKS, 3, NB, NB), BF16),
            pltpu.SemaphoreType.DMA((2 * CHUNKS + 2,)),
        ],
        compiler_params=params(28),
        name="encode",
    )(*map(in_hbm, (g2m_dest.T, inputs_t, embed_weight, send_weight, g2m_edges)))
    cuts = [(k, part) for k in range(4) for part in range(2)]
    return [
        dict(zip(cuts, lax.optimization_barrier([half[16 * k + 8 * part :][:8] for k, part in cuts])))
        for half in halves
    ]


def add(*values):
    total = values[0].astype(F32)
    for value in values[1:]:
        total = total + value.astype(F32)
    return total.astype(BF16)


def reduce(piece):
    both = range(2)
    links = Links()

    def far(part, step):
        return [links.send(piece[h][2, part], h, step) for h in both]

    def near(part, step, got):
        k = step % SIDE
        sent = []
        for h in both:
            value = piece[h][k, part]
            sent.append(links.send(value if got is None else add(value, got[h]), h, step))
        return sent

    def settled(part, at, up, down, *more):
        rows = slice(at * OWN, (at + 1) * OWN)
        values = [piece[h][0, part][rows] for h in both]
        return [
            add(values[h], up[h][rows], down[h][rows], *[m[h] for m in more]) for h in both
        ]

    far_0 = far(0, 1)
    down_0 = near(0, -1, None)
    up_0 = near(0, 1, far_0)
    far_1 = far(1, -1)
    sums_2 = settled(0, 0, up_0, down_0)
    from_2 = [links.send(sums_2[h], 1 - h, 1) for h in both]
    down_1 = near(1, -1, far_1)
    up_1 = near(1, 1, None)
    sums_1 = settled(0, 1, up_0, down_0, from_2)
    from_1 = [links.send(sums_1[h], 1 - h, 1) for h in both]
    sums_3 = settled(1, 1, up_1, down_1)
    from_3 = [links.send(sums_3[h], 1 - h, -1) for h in both]
    terms = []
    for h in both:
        terms += [piece[h][0, 1], up_1[h], down_1[h], from_1[h], from_3[h]]
    return terms


def start_kernel(*refs):
    terms, (encode_ref, message_ref, mesh_ref, *sent_refs) = refs[:10], refs[10:]
    total = None
    for h in range(2):
        value = None
        for term in terms[5 * h : 5 * h + 5]:
            term = term[:OWN].astype(F32)
            value = term if value is None else value + term
        act = silu(value).astype(BF16).reshape(OWN * NB, HALF)
        part = dot(act, encode_ref[h * HALF : (h + 1) * HALF, :])
        total = part if total is None else total + part
    mesh = total.astype(BF16)
    mesh_ref[...] = mesh
    put_sent(dot(mesh, message_ref[0]).astype(BF16), sent_refs)


def parity(axis):
    return lax.rem(lax.axis_index(axis), 2)


def put_sent(sent, refs):
    sent = sent.reshape(2, 2, NB, D)
    refs[0][...] = sent
    for at, axis in ((1, "grid"), (3, "mesh")):
        first, last = (sent[n] if axis == "grid" else sent[:, n] for n in range(2))
        even = parity(axis) == 0
        refs[at][...] = jnp.where(even, last, first)
        refs[at + 1][...] = jnp.where(even, first, last)


def sent_shapes():
    return [
        jax.ShapeDtypeStruct((OWN * NB, D), BF16),
        jax.ShapeDtypeStruct((2, 2, NB, D), BF16),
    ] + [jax.ShapeDtypeStruct((2, NB, D), BF16)] * 4


def mesh_start(terms, encode_weight, message_weight):
    return pl.pallas_call(
        start_kernel,
        out_shape=sent_shapes(),
        compiler_params=params(12),
        name="mesh_start",
    )(*terms, encode_weight, message_weight)


def step_kernel(layer, codes_ref, count_ref, mesh_ref, *rest):
    band, (couplings_ref, node_ref, next_ref), rest = rest[:7], rest[7:10], rest[10:]
    outs, (pad, normed) = rest[:-2], rest[-2:]
    own, col_a, col_b, row_a, row_b, corners_a, corners_b = band
    col = 3 - 3 * parity("mesh")
    row = 3 - 3 * parity("grid")
    for r in range(2):
        pad[4 * r + 5 : 4 * r + 7] = own[r]
        pad[4 * r + 4 + col] = col_a[r]
        pad[4 * r + 7 - col] = col_b[r]
    for at, middle, corners in ((row, row_a, corners_a), (3 - row, row_b, corners_b)):
        pad[pl.ds(4 * at + 1, 2)] = middle[...]
        pad[4 * at + col] = corners[0]
        pad[4 * at + 3 - col] = corners[1]
    for r in range(2):
        for c in range(2):
            near, weights = [], []
            for a in range(4):
                code = codes_ref[r * 2 + c, a]
                near.append(pad[(r + code // 3) * 4 + c + code % 3])
                live = (a < count_ref[r, c]).astype(BF16)
                weights.append(couplings_ref[r, c, a] * live)
            agg = dot_t(jnp.concatenate(weights, 0), jnp.concatenate(near, 0))
            act = silu(agg)
            scale = lax.rsqrt(jnp.mean(act * act, axis=-1, keepdims=True) + epsilon)
            at = (r * 2 + c) * NB
            normed[at : at + NB, :] = (act * scale).astype(BF16)
    mesh = (mesh_ref[...].astype(F32) + dot(normed[...], node_ref[layer])).astype(BF16)
    if layer == 0:
        outs[0][...] = mesh
        put_sent(dot(mesh, next_ref[1]).astype(BF16), outs[1:])
    else:
        proj = dot(mesh, next_ref[...]).astype(BF16).reshape(OWN, NB, D)
        outs[0][...] = proj[:, :, :HALF]
        outs[1][...] = proj[:, :, HALF:]


def mesh_step(layer, codes, count, mesh, band, couplings, node_weight, next_weight):
    if layer == 0:
        out_shape = sent_shapes()
    else:
        out_shape = [jax.ShapeDtypeStruct((OWN, NB, HALF), BF16)] * 2
    smem = pl.BlockSpec(memory_space=pltpu.SMEM)
    vmem = pl.BlockSpec(memory_space=pltpu.VMEM)
    return pl.pallas_call(
        functools.partial(step_kernel, layer),
        in_specs=[smem, smem] + [vmem] * 11,
        out_shape=out_shape,
        scratch_shapes=[pltpu.VMEM((16, NB, D), BF16), pltpu.VMEM((OWN * NB, D), BF16)],
        compiler_params=params(16),
        name="mesh_step",
    )(codes, count, mesh, *band, couplings, node_weight, next_weight)


def trade(value, axis, odd):
    size = lax.axis_size(axis)
    pairs = [(i, i + 1) for i in range(odd, size - 1, 2)]
    return lax.ppermute(value, axis, pairs + [(b, a) for a, b in pairs])


def band_of(own, row_a, row_b, col_a, col_b):
    col_a, col_b = trade(col_a, "mesh", 0), trade(col_b, "mesh", 1)
    row_a, row_b = trade(row_a, "grid", 0), trade(row_b, "grid", 1)
    corners = []
    for odd in range(2):
        row = 1 - (parity("grid") + odd) % 2
        ends = [lax.dynamic_slice_in_dim(value, row, 1, 0) for value in (col_a, col_b)]
        corners.append(trade(jnp.concatenate(ends, 0), "grid", odd))
    return own, col_a, col_b, row_a, row_b, *corners


BLOCKS = 8
STEPS = 3


def gather(owns):
    both = range(2)
    links = Links()
    near_1 = [links.send(owns[h], 1 - h, 1) for h in both]
    near_3 = [links.send(owns[h], 1 - h, -1) for h in both]
    part_0 = [jnp.concatenate([owns[h], near_1[h]], 0) for h in both]
    near_2 = [links.send(near_1[h], 1 - h, 1) for h in both]
    down_0 = [links.send(part_0[h], h, -1) for h in both]
    up_0 = [links.send(part_0[h], h, 1) for h in both]
    part_1 = [jnp.concatenate([near_2[h], near_3[h]], 0) for h in both]
    down_1 = [links.send(part_1[h], h, -1) for h in both]
    up_1 = [links.send(part_1[h], h, 1) for h in both]
    far_0 = [links.send(up_0[h], h, 1) for h in both]
    far_1 = [links.send(down_1[h], h, -1) for h in both]
    held = []
    for h in both:
        held += [part_0[h], part_1[h], up_0[h], up_1[h], far_0[h], far_1[h], down_0[h], down_1[h]]
    return held


def decode_kernel(src_ref, x_ref, edges_ref, output_ref, *rest):
    pieces, (out_ref, held, hidden, sems) = rest[:16], rest[16:]
    i = pl.program_id(0)

    @pl.when(i == 0)
    def _():
        copies = []
        for n in range(16):
            copy = pltpu.make_async_copy(
                pieces[n], held.at[n // 8, pl.ds(n % 8 * 8, 8)], sems.at[n]
            )
            copy.start()
            copies.append(copy)
        for copy in copies:
            copy.wait()

    me = lax.axis_index("mesh")
    my_y, my_z = me // SIDE, me % SIDE
    for b in range(BLOCKS):
        first, second = [], []
        for j in range(3):
            y, z, local = place(src_ref[j, i * BLOCKS + b])
            ky, kz = (my_y - y) & 3, (my_z - z) & 3
            first.append(held[0, (ky * SIDE + kz) * OWN + local])
            second.append(held[1, (kz * SIDE + ky) * OWN + local])
        edges = edges_ref[b].reshape(3 * NB, NB)
        for h, parts in enumerate((first, second)):
            decoded = dot_t(edges, jnp.concatenate(parts, 0))
            hidden[b * NB : (b + 1) * NB, h * HALF : (h + 1) * HALF] = silu(decoded).astype(BF16)
    total = lax.dot_general(
        output_ref[...], hidden[...], (((1,), (1,)), ((), ())), preferred_element_type=F32
    )
    out_ref[...] = (x_ref[...].astype(F32) + total).astype(BF16)


def decode(grid_inputs, m2g_src, m2g_edges, output_weight, pieces):
    rows = BLOCKS * NB
    inputs_t, output_t = grid_inputs.T, output_weight.T
    width = inputs_t.shape[0]
    result = pl.pallas_call(
        decode_kernel,
        grid_spec=pltpu.PrefetchScalarGridSpec(
            num_scalar_prefetch=1,
            grid=(STEPS,),
            in_specs=[
                pl.BlockSpec((width, rows), lambda i, *_: (0, i)),
                pl.BlockSpec((BLOCKS, 3, NB, NB), lambda i, *_: (i, 0, 0, 0)),
                pl.BlockSpec(output_t.shape, lambda i, *_: (0, 0)),
            ]
            + [pl.BlockSpec(memory_space=pl.ANY)] * 16,
            out_specs=pl.BlockSpec((width, rows), lambda i, *_: (0, i)),
            scratch_shapes=[
                pltpu.VMEM((2, 64, NB, HALF), BF16),
                pltpu.VMEM((rows, D), BF16),
                pltpu.SemaphoreType.DMA((16,)),
            ],
        ),
        out_shape=jax.ShapeDtypeStruct(inputs_t.shape, BF16),
        compiler_params=params(20),
        name="decode",
    )(m2g_src.T, inputs_t, m2g_edges, output_t, *pieces)
    return result.T


def per_device(
    grid_inputs,
    embed_weight,
    send_weight,
    g2m_dest,
    g2m_edges,
    encode_weight,
    adj_codes,
    adj_count,
    couplings,
    message_weight,
    node_weight,
    decode_weight,
    m2g_src,
    m2g_edges,
    output_weight,
):
    pieces = encode(grid_inputs, embed_weight, send_weight, g2m_dest, g2m_edges)
    mesh, *sent = mesh_start(reduce(pieces), encode_weight, message_weight)
    codes = adj_codes.reshape(OWN, -1)
    mesh, *sent = mesh_step(
        0, codes, adj_count, mesh, band_of(*sent), couplings, node_weight, message_weight
    )
    owns = mesh_step(
        1, codes, adj_count, mesh, band_of(*sent), couplings, node_weight, decode_weight
    )
    return decode(grid_inputs, m2g_src, m2g_edges, output_weight, gather(owns))


def solution(mesh):
    placed = (
        P(("grid", "mesh"), None),
        P(),
        P(),
        P(("grid", "mesh"), None),
        P(("grid", "mesh"), None, None, None),
        P(),
        P("grid", "mesh", None),
        P("grid", "mesh"),
        P("grid", "mesh", None, None, None),
        P(),
        P(),
        P(),
        P(("grid", "mesh"), None),
        P(("grid", "mesh"), None, None, None),
        P(),
    )
    return jax.shard_map(
        per_device, mesh=mesh, in_specs=placed, out_specs=P(("grid", "mesh"), None), check_vma=False
    )
```

```python
import functools

import jax
import jax.numpy as jnp
from jax import lax
from jax.experimental import pallas as pl
from jax.experimental.pallas import tpu as pltpu
from jax.sharding import PartitionSpec as P

epsilon = 1e-05
BF16 = jnp.bfloat16
F32 = jnp.float32
SIDE = 4
NB = 128
D = 512
HALF = 256
OWN = 4


def params(mib):
    return pltpu.CompilerParams(vmem_limit_bytes=mib * 1024 * 1024)


def dot(a, b):
    return jnp.dot(a, b, preferred_element_type=F32)


def dot_t(a, b):
    return lax.dot_general(a, b, (((0,), (0,)), ((), ())), preferred_element_type=F32)


def silu(v):
    half = 0.5 * v
    return half + half * jnp.tanh(half)


def shift(value, axis, step):
    pairs = []
    for y in range(SIDE):
        for z in range(SIDE):
            to = ((y + step) % SIDE, z) if axis == 0 else (y, (z + step) % SIDE)
            pairs.append((y * SIDE + z, to[0] * SIDE + to[1]))
    return lax.ppermute(value, "mesh", pairs)


class Links:
    def __init__(self):
        self.last = {}

    def send(self, value, axis, step):
        link = (axis, step)
        if link in self.last:
            value, _ = lax.optimization_barrier((value, self.last[link]))
        self.last[link] = shift(value, axis, step)
        return self.last[link]


def place(code):
    row = code // 32
    col = code % 32
    owner = col // 2
    return owner // SIDE, owner % SIDE, row * 2 + col % 2


CHUNKS = 3
CHUNK_BLOCKS = 8
CHUNK = CHUNK_BLOCKS * NB


def encode_kernel(dest_ref, x_hbm, embed_hbm, send_hbm, edges_hbm, out_0, out_1, x, embed, send, edges, sems):
    def inputs(c):
        return (
            pltpu.make_async_copy(
                x_hbm.at[:, pl.ds(pl.multiple_of(c * CHUNK, CHUNK), CHUNK)], x.at[c], sems.at[2 * c + 2]
            ),
            pltpu.make_async_copy(
                edges_hbm.at[pl.ds(c * CHUNK_BLOCKS, CHUNK_BLOCKS)], edges.at[c], sems.at[2 * c + 3]
            ),
        )

    weights = (
        pltpu.make_async_copy(embed_hbm, embed, sems.at[0]),
        pltpu.make_async_copy(send_hbm, send, sems.at[1]),
    )
    for copy in weights + inputs(0):
        copy.start()

    @pl.loop(1, CHUNKS)
    def _(c):
        for copy in inputs(c):
            copy.start()

    @pl.loop(0, 64)
    def _(n):
        out_0[n] = jnp.zeros((NB, HALF), BF16)
        out_1[n] = jnp.zeros((NB, HALF), BF16)

    me = lax.axis_index("mesh")
    my_y, my_z = me // SIDE, me % SIDE
    for copy in weights:
        copy.wait()

    @pl.loop(0, CHUNKS)
    def _(c):
        for copy in inputs(c):
            copy.wait()
        latent = silu(dot_t(x[c], embed[...])).astype(BF16)
        proj = dot(latent, send[...]).astype(BF16)
        for b in range(CHUNK_BLOCKS):
            both = jnp.concatenate([edges[c, b, j] for j in range(3)], 1)
            message = dot_t(both, proj[b * NB : (b + 1) * NB])
            for j in range(3):
                y, z, local = place(dest_ref[j, c * CHUNK_BLOCKS + b])
                dy, dz = (y - my_y) & 3, (z - my_z) & 3
                part = message[j * NB : (j + 1) * NB]
                at_0 = (dy * SIDE + ((2 - dz) & 3)) * OWN + local
                at_1 = (dz * SIDE + ((2 - dy) & 3)) * OWN + local
                out_0[at_0] = (out_0[at_0].astype(F32) + part[:, :HALF]).astype(BF16)
                out_1[at_1] = (out_1[at_1].astype(F32) + part[:, HALF:]).astype(BF16)


def in_hbm(value):
    return pltpu.with_memory_space_constraint(value, pltpu.HBM)


def encode(grid_inputs, embed_weight, send_weight, g2m_dest, g2m_edges):
    inputs_t = grid_inputs.T
    width = inputs_t.shape[0]
    halves = pl.pallas_call(
        encode_kernel,
        in_specs=[pl.BlockSpec(memory_space=pltpu.SMEM)] + [pl.BlockSpec(memory_space=pltpu.HBM)] * 4,
        out_specs=[pl.BlockSpec(memory_space=pltpu.VMEM)] * 2,
        out_shape=[pltpu.VMEM((64, NB, HALF), BF16)] * 2,
        scratch_shapes=[
            pltpu.VMEM((CHUNKS, width, CHUNK), BF16),
            pltpu.VMEM(embed_weight.shape, BF16),
            pltpu.VMEM(send_weight.shape, BF16),
            pltpu.VMEM((CHUNKS, CHUNK_BLOCKS, 3, NB, NB), BF16),
            pltpu.SemaphoreType.DMA((2 * CHUNKS + 2,)),
        ],
        compiler_params=params(28),
        name="encode",
    )(*map(in_hbm, (g2m_dest.T, inputs_t, embed_weight, send_weight, g2m_edges)))
    cuts = [(k, part) for k in range(4) for part in range(2)]
    return [
        dict(zip(cuts, lax.optimization_barrier([half[16 * k + 8 * part :][:8] for k, part in cuts])))
        for half in halves
    ]


def add(*values):
    total = values[0].astype(F32)
    for value in values[1:]:
        total = total + value.astype(F32)
    return total.astype(BF16)


def reduce(piece):
    both = range(2)
    links = Links()

    def far(part, step):
        return [links.send(piece[h][2, part], h, step) for h in both]

    def near(part, step, got):
        k = step % SIDE
        sent = []
        for h in both:
            value = piece[h][k, part]
            sent.append(links.send(value if got is None else add(value, got[h]), h, step))
        return sent

    def settled(part, at, up, down, *more):
        rows = slice(at * OWN, (at + 1) * OWN)
        values = [piece[h][0, part][rows] for h in both]
        return [
            add(values[h], up[h][rows], down[h][rows], *[m[h] for m in more]) for h in both
        ]

    far_0 = far(0, 1)
    down_0 = near(0, -1, None)
    up_0 = near(0, 1, far_0)
    far_1 = far(1, -1)
    sums_2 = settled(0, 0, up_0, down_0)
    from_2 = [links.send(sums_2[h], 1 - h, 1) for h in both]
    down_1 = near(1, -1, far_1)
    up_1 = near(1, 1, None)
    sums_1 = settled(0, 1, up_0, down_0, from_2)
    from_1 = [links.send(sums_1[h], 1 - h, 1) for h in both]
    sums_3 = settled(1, 1, up_1, down_1)
    from_3 = [links.send(sums_3[h], 1 - h, -1) for h in both]
    terms = []
    for h in both:
        terms += [piece[h][0, 1], up_1[h], down_1[h], from_1[h], from_3[h]]
    return terms


def start_kernel(*refs):
    terms, (encode_ref, message_ref, mesh_ref, *sent_refs) = refs[:10], refs[10:]
    total = None
    for h in range(2):
        value = None
        for term in terms[5 * h : 5 * h + 5]:
            term = term[:OWN].astype(F32)
            value = term if value is None else value + term
        act = silu(value).astype(BF16).reshape(OWN * NB, HALF)
        part = dot(act, encode_ref[h * HALF : (h + 1) * HALF, :])
        total = part if total is None else total + part
    mesh = total.astype(BF16)
    mesh_ref[...] = mesh
    put_sent(dot(mesh, message_ref[0]).astype(BF16), sent_refs)


def parity(axis):
    return lax.rem(lax.axis_index(axis), 2)


def put_sent(sent, refs):
    sent = sent.reshape(2, 2, NB, D)
    refs[0][...] = sent
    for at, axis in ((1, "grid"), (3, "mesh")):
        first, last = (sent[n] if axis == "grid" else sent[:, n] for n in range(2))
        even = parity(axis) == 0
        refs[at][...] = jnp.where(even, last, first)
        refs[at + 1][...] = jnp.where(even, first, last)


def sent_shapes():
    return [
        jax.ShapeDtypeStruct((OWN * NB, D), BF16),
        jax.ShapeDtypeStruct((2, 2, NB, D), BF16),
    ] + [jax.ShapeDtypeStruct((2, NB, D), BF16)] * 4


def mesh_start(terms, encode_weight, message_weight):
    return pl.pallas_call(
        start_kernel,
        out_shape=sent_shapes(),
        compiler_params=params(12),
        name="mesh_start",
    )(*terms, encode_weight, message_weight)


def step_kernel(layer, codes_ref, count_ref, mesh_ref, *rest):
    band, (couplings_ref, node_ref, next_ref), rest = rest[:7], rest[7:10], rest[10:]
    outs, (pad, normed) = rest[:-2], rest[-2:]
    own, col_a, col_b, row_a, row_b, corners_a, corners_b = band
    col = 3 - 3 * parity("mesh")
    row = 3 - 3 * parity("grid")
    for r in range(2):
        pad[4 * r + 5 : 4 * r + 7] = own[r]
        pad[4 * r + 4 + col] = col_a[r]
        pad[4 * r + 7 - col] = col_b[r]
    for at, middle, corners in ((row, row_a, corners_a), (3 - row, row_b, corners_b)):
        pad[pl.ds(4 * at + 1, 2)] = middle[...]
        pad[4 * at + col] = corners[0]
        pad[4 * at + 3 - col] = corners[1]
    for r in range(2):
        for c in range(2):
            near, weights = [], []
            for a in range(4):
                code = codes_ref[r * 2 + c, a]
                near.append(pad[(r + code // 3) * 4 + c + code % 3])
                live = (a < count_ref[r, c]).astype(BF16)
                weights.append(couplings_ref[r, c, a] * live)
            agg = dot_t(jnp.concatenate(weights, 0), jnp.concatenate(near, 0))
            act = silu(agg)
            scale = lax.rsqrt(jnp.mean(act * act, axis=-1, keepdims=True) + epsilon)
            at = (r * 2 + c) * NB
            normed[at : at + NB, :] = (act * scale).astype(BF16)
    mesh = (mesh_ref[...].astype(F32) + dot(normed[...], node_ref[layer])).astype(BF16)
    if layer == 0:
        outs[0][...] = mesh
        put_sent(dot(mesh, next_ref[1]).astype(BF16), outs[1:])
    else:
        proj = dot(mesh, next_ref[...]).astype(BF16).reshape(OWN, NB, D)
        outs[0][...] = proj[:, :, :HALF]
        outs[1][...] = proj[:, :, HALF:]


def mesh_step(layer, codes, count, mesh, band, couplings, node_weight, next_weight):
    if layer == 0:
        out_shape = sent_shapes()
    else:
        out_shape = [jax.ShapeDtypeStruct((OWN, NB, HALF), BF16)] * 2
    smem = pl.BlockSpec(memory_space=pltpu.SMEM)
    vmem = pl.BlockSpec(memory_space=pltpu.VMEM)
    return pl.pallas_call(
        functools.partial(step_kernel, layer),
        in_specs=[smem, smem] + [vmem] * 11,
        out_shape=out_shape,
        scratch_shapes=[pltpu.VMEM((16, NB, D), BF16), pltpu.VMEM((OWN * NB, D), BF16)],
        compiler_params=params(16),
        name="mesh_step",
    )(codes, count, mesh, *band, couplings, node_weight, next_weight)


def trade(value, axis, odd):
    size = lax.axis_size(axis)
    pairs = [(i, i + 1) for i in range(odd, size - 1, 2)]
    return lax.ppermute(value, axis, pairs + [(b, a) for a, b in pairs])


def band_of(ends, own, row_a, row_b, col_a, col_b):
    col_a, col_b = trade(col_a, "mesh", 0), trade(col_b, "mesh", 1)
    row_a, row_b = trade(row_a, "grid", 0), trade(row_b, "grid", 1)
    corners = []
    for odd in range(2):
        parts = [lax.dynamic_slice(col, ends[odd], (1, NB, D)) for col in (col_a, col_b)]
        corners.append(trade(jnp.concatenate(parts, 0), "grid", odd))
    return own, col_a, col_b, row_a, row_b, *corners


BLOCKS = 8
STEPS = 3


def gather(owns):
    both = range(2)
    links = Links()
    near_1 = [links.send(owns[h], 1 - h, 1) for h in both]
    near_3 = [links.send(owns[h], 1 - h, -1) for h in both]
    part_0 = [jnp.concatenate([owns[h], near_1[h]], 0) for h in both]
    near_2 = [links.send(near_1[h], 1 - h, 1) for h in both]
    down_0 = [links.send(part_0[h], h, -1) for h in both]
    up_0 = [links.send(part_0[h], h, 1) for h in both]
    part_1 = [jnp.concatenate([near_2[h], near_3[h]], 0) for h in both]
    down_1 = [links.send(part_1[h], h, -1) for h in both]
    up_1 = [links.send(part_1[h], h, 1) for h in both]
    far_0 = [links.send(up_0[h], h, 1) for h in both]
    far_1 = [links.send(down_1[h], h, -1) for h in both]
    held = []
    for h in both:
        held += [part_0[h], part_1[h], up_0[h], up_1[h], far_0[h], far_1[h], down_0[h], down_1[h]]
    return held


def decode_kernel(src_ref, x_ref, edges_ref, output_ref, *rest):
    pieces, (out_ref, held, hidden, sems) = rest[:16], rest[16:]
    i = pl.program_id(0)

    @pl.when(i == 0)
    def _():
        copies = []
        for n in range(16):
            copy = pltpu.make_async_copy(
                pieces[n], held.at[n // 8, pl.ds(n % 8 * 8, 8)], sems.at[n]
            )
            copy.start()
            copies.append(copy)
        for copy in copies:
            copy.wait()

    me = lax.axis_index("mesh")
    my_y, my_z = me // SIDE, me % SIDE
    for b in range(BLOCKS):
        first, second = [], []
        for j in range(3):
            y, z, local = place(src_ref[j, i * BLOCKS + b])
            ky, kz = (my_y - y) & 3, (my_z - z) & 3
            first.append(held[0, (ky * SIDE + kz) * OWN + local])
            second.append(held[1, (kz * SIDE + ky) * OWN + local])
        edges = edges_ref[b].reshape(3 * NB, NB)
        for h, parts in enumerate((first, second)):
            decoded = dot_t(edges, jnp.concatenate(parts, 0))
            hidden[b * NB : (b + 1) * NB, h * HALF : (h + 1) * HALF] = silu(decoded).astype(BF16)
    total = lax.dot_general(
        output_ref[...], hidden[...], (((1,), (1,)), ((), ())), preferred_element_type=F32
    )
    out_ref[...] = (x_ref[...].astype(F32) + total).astype(BF16)


def decode(grid_inputs, m2g_src, m2g_edges, output_weight, pieces):
    rows = BLOCKS * NB
    inputs_t, output_t = grid_inputs.T, output_weight.T
    width = inputs_t.shape[0]
    result = pl.pallas_call(
        decode_kernel,
        grid_spec=pltpu.PrefetchScalarGridSpec(
            num_scalar_prefetch=1,
            grid=(STEPS,),
            in_specs=[
                pl.BlockSpec((width, rows), lambda i, *_: (0, i)),
                pl.BlockSpec((BLOCKS, 3, NB, NB), lambda i, *_: (i, 0, 0, 0)),
                pl.BlockSpec(output_t.shape, lambda i, *_: (0, 0)),
            ]
            + [pl.BlockSpec(memory_space=pl.ANY)] * 16,
            out_specs=pl.BlockSpec((width, rows), lambda i, *_: (0, i)),
            scratch_shapes=[
                pltpu.VMEM((2, 64, NB, HALF), BF16),
                pltpu.VMEM((rows, D), BF16),
                pltpu.SemaphoreType.DMA((16,)),
            ],
        ),
        out_shape=jax.ShapeDtypeStruct(inputs_t.shape, BF16),
        compiler_params=params(20),
        name="decode",
    )(m2g_src.T, inputs_t, m2g_edges, output_t, *pieces)
    return result.T


def per_device(
    grid_inputs,
    embed_weight,
    send_weight,
    g2m_dest,
    g2m_edges,
    encode_weight,
    adj_codes,
    adj_count,
    couplings,
    message_weight,
    node_weight,
    decode_weight,
    m2g_src,
    m2g_edges,
    output_weight,
):
    zero = jnp.uint32(0)
    odd = parity("grid").astype(jnp.uint32)
    ends = [(1 - odd, zero, zero), (odd, zero, zero)]
    g2m_dest, ends = lax.optimization_barrier((g2m_dest, ends))
    pieces = encode(grid_inputs, embed_weight, send_weight, g2m_dest, g2m_edges)
    mesh, *sent = mesh_start(reduce(pieces), encode_weight, message_weight)
    codes = adj_codes.reshape(OWN, -1)
    mesh, *sent = mesh_step(
        0, codes, adj_count, mesh, band_of(ends, *sent), couplings, node_weight, message_weight
    )
    owns = mesh_step(
        1, codes, adj_count, mesh, band_of(ends, *sent), couplings, node_weight, decode_weight
    )
    return decode(grid_inputs, m2g_src, m2g_edges, output_weight, gather(owns))


def solution(mesh):
    placed = (
        P(("grid", "mesh"), None),
        P(),
        P(),
        P(("grid", "mesh"), None),
        P(("grid", "mesh"), None, None, None),
        P(),
        P("grid", "mesh", None),
        P("grid", "mesh"),
        P("grid", "mesh", None, None, None),
        P(),
        P(),
        P(),
        P(("grid", "mesh"), None),
        P(("grid", "mesh"), None, None, None),
        P(),
    )
    return jax.shard_map(
        per_device, mesh=mesh, in_specs=placed, out_specs=P(("grid", "mesh"), None), check_vma=False
    )
```

```python
import functools

import jax
import jax.numpy as jnp
from jax import lax
from jax.experimental import pallas as pl
from jax.experimental.pallas import tpu as pltpu
from jax.sharding import PartitionSpec as P

epsilon = 1e-05
BF16 = jnp.bfloat16
F32 = jnp.float32
SIDE = 4
NB = 128
D = 512
HALF = 256
OWN = 4


def params(mib):
    return pltpu.CompilerParams(vmem_limit_bytes=mib * 1024 * 1024)


def dot(a, b):
    return jnp.dot(a, b, preferred_element_type=F32)


def dot_t(a, b):
    return lax.dot_general(a, b, (((0,), (0,)), ((), ())), preferred_element_type=F32)


def silu(v):
    half = 0.5 * v
    return half + half * jnp.tanh(half)


def shift(value, axis, step):
    pairs = []
    for y in range(SIDE):
        for z in range(SIDE):
            to = ((y + step) % SIDE, z) if axis == 0 else (y, (z + step) % SIDE)
            pairs.append((y * SIDE + z, to[0] * SIDE + to[1]))
    return lax.ppermute(value, "mesh", pairs)


class Links:
    def __init__(self):
        self.last = {}

    def send(self, value, axis, step):
        link = (axis, step)
        if link in self.last:
            value, _ = lax.optimization_barrier((value, self.last[link]))
        self.last[link] = shift(value, axis, step)
        return self.last[link]


def place(code):
    row = code // 32
    col = code % 32
    owner = col // 2
    return owner // SIDE, owner % SIDE, row * 2 + col % 2


CHUNKS = 3
CHUNK_BLOCKS = 8
CHUNK = CHUNK_BLOCKS * NB


def encode_kernel(dest_ref, x_hbm, embed_hbm, send_hbm, edges_hbm, out_0, out_1, x, embed, send, edges, sems):
    def inputs(c):
        return (
            pltpu.make_async_copy(
                x_hbm.at[:, pl.ds(pl.multiple_of(c * CHUNK, CHUNK), CHUNK)], x.at[c], sems.at[2 * c + 2]
            ),
            pltpu.make_async_copy(
                edges_hbm.at[pl.ds(c * CHUNK_BLOCKS, CHUNK_BLOCKS)], edges.at[c], sems.at[2 * c + 3]
            ),
        )

    weights = (
        pltpu.make_async_copy(embed_hbm, embed, sems.at[0]),
        pltpu.make_async_copy(send_hbm, send, sems.at[1]),
    )
    for copy in weights + inputs(0):
        copy.start()

    @pl.loop(1, CHUNKS)
    def _(c):
        for copy in inputs(c):
            copy.start()

    @pl.loop(0, 64)
    def _(n):
        out_0[n] = jnp.zeros((NB, HALF), BF16)
        out_1[n] = jnp.zeros((NB, HALF), BF16)

    me = lax.axis_index("mesh")
    my_y, my_z = me // SIDE, me % SIDE
    for copy in weights:
        copy.wait()

    @pl.loop(0, CHUNKS)
    def _(c):
        for copy in inputs(c):
            copy.wait()
        latent = silu(dot_t(x[c], embed[...])).astype(BF16)
        proj = dot(latent, send[...]).astype(BF16)
        for b in range(CHUNK_BLOCKS):
            both = jnp.concatenate([edges[c, b, j] for j in range(3)], 1)
            message = dot_t(both, proj[b * NB : (b + 1) * NB])
            for j in range(3):
                y, z, local = place(dest_ref[j, c * CHUNK_BLOCKS + b])
                dy, dz = (y - my_y) & 3, (z - my_z) & 3
                part = message[j * NB : (j + 1) * NB]
                at_0 = (dy * SIDE + ((2 - dz) & 3)) * OWN + local
                at_1 = (dz * SIDE + ((2 - dy) & 3)) * OWN + local
                out_0[at_0] = (out_0[at_0].astype(F32) + part[:, :HALF]).astype(BF16)
                out_1[at_1] = (out_1[at_1].astype(F32) + part[:, HALF:]).astype(BF16)


def in_hbm(value):
    return pltpu.with_memory_space_constraint(value, pltpu.HBM)


def encode(grid_inputs, embed_weight, send_weight, g2m_dest, g2m_edges):
    inputs_t = grid_inputs.T
    width = inputs_t.shape[0]
    halves = pl.pallas_call(
        encode_kernel,
        in_specs=[pl.BlockSpec(memory_space=pltpu.SMEM)] + [pl.BlockSpec(memory_space=pltpu.HBM)] * 4,
        out_specs=[pl.BlockSpec(memory_space=pltpu.VMEM)] * 2,
        out_shape=[pltpu.VMEM((64, NB, HALF), BF16)] * 2,
        scratch_shapes=[
            pltpu.VMEM((CHUNKS, width, CHUNK), BF16),
            pltpu.VMEM(embed_weight.shape, BF16),
            pltpu.VMEM(send_weight.shape, BF16),
            pltpu.VMEM((CHUNKS, CHUNK_BLOCKS, 3, NB, NB), BF16),
            pltpu.SemaphoreType.DMA((2 * CHUNKS + 2,)),
        ],
        compiler_params=params(28),
        name="encode",
    )(*map(in_hbm, (g2m_dest.T, inputs_t, embed_weight, send_weight, g2m_edges)))
    early = ((2, 0), (3, 0), (2, 1))
    late = [(k, part) for k in range(4) for part in range(2) if (k, part) not in early]
    pieces = [{}, {}]
    for cuts in (early, late):
        values = [[half[16 * k + 8 * part :][:8] for k, part in cuts] for half in halves]
        for piece, cut in zip(pieces, lax.optimization_barrier(values)):
            piece.update(zip(cuts, cut))
    return pieces


def add(*values):
    total = values[0].astype(F32)
    for value in values[1:]:
        total = total + value.astype(F32)
    return total.astype(BF16)


def reduce(piece):
    both = range(2)
    links = Links()

    def far(part, step):
        return [links.send(piece[h][2, part], h, step) for h in both]

    def near(part, step, got):
        k = step % SIDE
        sent = []
        for h in both:
            value = piece[h][k, part]
            sent.append(links.send(value if got is None else add(value, got[h]), h, step))
        return sent

    def settled(part, at, up, down, *more):
        rows = slice(at * OWN, (at + 1) * OWN)
        values = [piece[h][0, part][rows] for h in both]
        return [
            add(values[h], up[h][rows], down[h][rows], *[m[h] for m in more]) for h in both
        ]

    far_0 = far(0, 1)
    down_0 = near(0, -1, None)
    up_0 = near(0, 1, far_0)
    far_1 = far(1, -1)
    sums_2 = settled(0, 0, up_0, down_0)
    from_2 = [links.send(sums_2[h], 1 - h, 1) for h in both]
    down_1 = near(1, -1, far_1)
    up_1 = near(1, 1, None)
    sums_1 = settled(0, 1, up_0, down_0, from_2)
    from_1 = [links.send(sums_1[h], 1 - h, 1) for h in both]
    sums_3 = settled(1, 1, up_1, down_1)
    from_3 = [links.send(sums_3[h], 1 - h, -1) for h in both]
    terms = []
    for h in both:
        terms += [piece[h][0, 1], up_1[h], down_1[h], from_1[h], from_3[h]]
    return terms


def start_kernel(*refs):
    terms, (encode_ref, message_ref, mesh_ref, *sent_refs) = refs[:10], refs[10:]
    total = None
    for h in range(2):
        value = None
        for term in terms[5 * h : 5 * h + 5]:
            term = term[:OWN].astype(F32)
            value = term if value is None else value + term
        act = silu(value).astype(BF16).reshape(OWN * NB, HALF)
        part = dot(act, encode_ref[h * HALF : (h + 1) * HALF, :])
        total = part if total is None else total + part
    mesh = total.astype(BF16)
    mesh_ref[...] = mesh
    put_sent(dot(mesh, message_ref[0]).astype(BF16), sent_refs)


def parity(axis):
    return lax.rem(lax.axis_index(axis), 2)


def put_sent(sent, refs):
    sent = sent.reshape(2, 2, NB, D)
    refs[0][...] = sent
    for at, axis in ((1, "grid"), (3, "mesh")):
        first, last = (sent[n] if axis == "grid" else sent[:, n] for n in range(2))
        even = parity(axis) == 0
        refs[at][...] = jnp.where(even, last, first)
        refs[at + 1][...] = jnp.where(even, first, last)


def sent_shapes():
    return [
        jax.ShapeDtypeStruct((OWN * NB, D), BF16),
        jax.ShapeDtypeStruct((2, 2, NB, D), BF16),
    ] + [jax.ShapeDtypeStruct((2, NB, D), BF16)] * 4


def mesh_start(terms, encode_weight, message_weight):
    return pl.pallas_call(
        start_kernel,
        out_shape=sent_shapes(),
        compiler_params=params(12),
        name="mesh_start",
    )(*terms, encode_weight, message_weight)


def step_kernel(layer, codes_ref, count_ref, mesh_ref, *rest):
    band, (couplings_ref, node_ref, next_ref), rest = rest[:7], rest[7:10], rest[10:]
    outs, (pad, normed) = rest[:-2], rest[-2:]
    own, col_a, col_b, row_a, row_b, corners_a, corners_b = band
    col = 3 - 3 * parity("mesh")
    row = 3 - 3 * parity("grid")
    for r in range(2):
        pad[4 * r + 5 : 4 * r + 7] = own[r]
        pad[4 * r + 4 + col] = col_a[r]
        pad[4 * r + 7 - col] = col_b[r]
    for at, middle, corners in ((row, row_a, corners_a), (3 - row, row_b, corners_b)):
        pad[pl.ds(4 * at + 1, 2)] = middle[...]
        pad[4 * at + col] = corners[0]
        pad[4 * at + 3 - col] = corners[1]
    for r in range(2):
        for c in range(2):
            near, weights = [], []
            for a in range(4):
                code = codes_ref[r * 2 + c, a]
                near.append(pad[(r + code // 3) * 4 + c + code % 3])
                live = (a < count_ref[r, c]).astype(BF16)
                weights.append(couplings_ref[r, c, a] * live)
            agg = dot_t(jnp.concatenate(weights, 0), jnp.concatenate(near, 0))
            act = silu(agg)
            scale = lax.rsqrt(jnp.mean(act * act, axis=-1, keepdims=True) + epsilon)
            at = (r * 2 + c) * NB
            normed[at : at + NB, :] = (act * scale).astype(BF16)
    mesh = (mesh_ref[...].astype(F32) + dot(normed[...], node_ref[layer])).astype(BF16)
    if layer == 0:
        outs[0][...] = mesh
        put_sent(dot(mesh, next_ref[1]).astype(BF16), outs[1:])
    else:
        proj = dot(mesh, next_ref[...]).astype(BF16).reshape(OWN, NB, D)
        outs[0][...] = proj[:, :, :HALF]
        outs[1][...] = proj[:, :, HALF:]


def mesh_step(layer, codes, count, mesh, band, couplings, node_weight, next_weight):
    if layer == 0:
        out_shape = sent_shapes()
    else:
        out_shape = [jax.ShapeDtypeStruct((OWN, NB, HALF), BF16)] * 2
    smem = pl.BlockSpec(memory_space=pltpu.SMEM)
    vmem = pl.BlockSpec(memory_space=pltpu.VMEM)
    return pl.pallas_call(
        functools.partial(step_kernel, layer),
        in_specs=[smem, smem] + [vmem] * 11,
        out_shape=out_shape,
        scratch_shapes=[pltpu.VMEM((16, NB, D), BF16), pltpu.VMEM((OWN * NB, D), BF16)],
        compiler_params=params(16),
        name="mesh_step",
    )(codes, count, mesh, *band, couplings, node_weight, next_weight)


def trade(value, axis, odd):
    size = lax.axis_size(axis)
    pairs = [(i, i + 1) for i in range(odd, size - 1, 2)]
    return lax.ppermute(value, axis, pairs + [(b, a) for a, b in pairs])


def band_of(ends, own, row_a, row_b, col_a, col_b):
    col_a, col_b = trade(col_a, "mesh", 0), trade(col_b, "mesh", 1)
    row_a, row_b = trade(row_a, "grid", 0), trade(row_b, "grid", 1)
    corners = []
    for odd in range(2):
        parts = [lax.dynamic_slice(col, ends[odd], (1, NB, D)) for col in (col_a, col_b)]
        corners.append(trade(jnp.concatenate(parts, 0), "grid", odd))
    return own, col_a, col_b, row_a, row_b, *corners


BLOCKS = 8
STEPS = 3


def gather(owns):
    both = range(2)
    links = Links()
    near_1 = [links.send(owns[h], 1 - h, 1) for h in both]
    near_3 = [links.send(owns[h], 1 - h, -1) for h in both]
    part_0 = [jnp.concatenate([owns[h], near_1[h]], 0) for h in both]
    near_2 = [links.send(near_1[h], 1 - h, 1) for h in both]
    down_0 = [links.send(part_0[h], h, -1) for h in both]
    up_0 = [links.send(part_0[h], h, 1) for h in both]
    part_1 = [jnp.concatenate([near_2[h], near_3[h]], 0) for h in both]
    down_1 = [links.send(part_1[h], h, -1) for h in both]
    up_1 = [links.send(part_1[h], h, 1) for h in both]
    far_0 = [links.send(up_0[h], h, 1) for h in both]
    far_1 = [links.send(down_1[h], h, -1) for h in both]
    held = []
    for h in both:
        held += [part_0[h], part_1[h], up_0[h], up_1[h], far_0[h], far_1[h], down_0[h], down_1[h]]
    return held


def decode_kernel(src_ref, x_ref, edges_ref, output_ref, *rest):
    pieces, (out_ref, held, hidden, sems) = rest[:16], rest[16:]
    i = pl.program_id(0)

    @pl.when(i == 0)
    def _():
        copies = []
        for n in range(16):
            copy = pltpu.make_async_copy(
                pieces[n], held.at[n // 8, pl.ds(n % 8 * 8, 8)], sems.at[n]
            )
            copy.start()
            copies.append(copy)
        for copy in copies:
            copy.wait()

    me = lax.axis_index("mesh")
    my_y, my_z = me // SIDE, me % SIDE
    for b in range(BLOCKS):
        first, second = [], []
        for j in range(3):
            y, z, local = place(src_ref[j, i * BLOCKS + b])
            ky, kz = (my_y - y) & 3, (my_z - z) & 3
            first.append(held[0, (ky * SIDE + kz) * OWN + local])
            second.append(held[1, (kz * SIDE + ky) * OWN + local])
        edges = edges_ref[b].reshape(3 * NB, NB)
        for h, parts in enumerate((first, second)):
            decoded = dot_t(edges, jnp.concatenate(parts, 0))
            hidden[b * NB : (b + 1) * NB, h * HALF : (h + 1) * HALF] = silu(decoded).astype(BF16)
    total = lax.dot_general(
        output_ref[...], hidden[...], (((1,), (1,)), ((), ())), preferred_element_type=F32
    )
    out_ref[...] = (x_ref[...].astype(F32) + total).astype(BF16)


def decode(grid_inputs, m2g_src, m2g_edges, output_weight, pieces):
    rows = BLOCKS * NB
    inputs_t, output_t = grid_inputs.T, output_weight.T
    width = inputs_t.shape[0]
    result = pl.pallas_call(
        decode_kernel,
        grid_spec=pltpu.PrefetchScalarGridSpec(
            num_scalar_prefetch=1,
            grid=(STEPS,),
            in_specs=[
                pl.BlockSpec((width, rows), lambda i, *_: (0, i)),
                pl.BlockSpec((BLOCKS, 3, NB, NB), lambda i, *_: (i, 0, 0, 0)),
                pl.BlockSpec(output_t.shape, lambda i, *_: (0, 0)),
            ]
            + [pl.BlockSpec(memory_space=pl.ANY)] * 16,
            out_specs=pl.BlockSpec((width, rows), lambda i, *_: (0, i)),
            scratch_shapes=[
                pltpu.VMEM((2, 64, NB, HALF), BF16),
                pltpu.VMEM((rows, D), BF16),
                pltpu.SemaphoreType.DMA((16,)),
            ],
        ),
        out_shape=jax.ShapeDtypeStruct(inputs_t.shape, BF16),
        compiler_params=params(20),
        name="decode",
    )(m2g_src.T, inputs_t, m2g_edges, output_t, *pieces)
    return result.T


def per_device(
    grid_inputs,
    embed_weight,
    send_weight,
    g2m_dest,
    g2m_edges,
    encode_weight,
    adj_codes,
    adj_count,
    couplings,
    message_weight,
    node_weight,
    decode_weight,
    m2g_src,
    m2g_edges,
    output_weight,
):
    zero = jnp.uint32(0)
    odd = parity("grid").astype(jnp.uint32)
    ends = [(1 - odd, zero, zero), (odd, zero, zero)]
    g2m_dest, ends = lax.optimization_barrier((g2m_dest, ends))
    pieces = encode(grid_inputs, embed_weight, send_weight, g2m_dest, g2m_edges)
    mesh, *sent = mesh_start(reduce(pieces), encode_weight, message_weight)
    codes = adj_codes.reshape(OWN, -1)
    mesh, *sent = mesh_step(
        0, codes, adj_count, mesh, band_of(ends, *sent), couplings, node_weight, message_weight
    )
    owns = mesh_step(
        1, codes, adj_count, mesh, band_of(ends, *sent), couplings, node_weight, decode_weight
    )
    return decode(grid_inputs, m2g_src, m2g_edges, output_weight, gather(owns))


def solution(mesh):
    placed = (
        P(("grid", "mesh"), None),
        P(),
        P(),
        P(("grid", "mesh"), None),
        P(("grid", "mesh"), None, None, None),
        P(),
        P("grid", "mesh", None),
        P("grid", "mesh"),
        P("grid", "mesh", None, None, None),
        P(),
        P(),
        P(),
        P(("grid", "mesh"), None),
        P(("grid", "mesh"), None, None, None),
        P(),
    )
    return jax.shard_map(
        per_device, mesh=mesh, in_specs=placed, out_specs=P(("grid", "mesh"), None), check_vma=False
    )
```
